256 devices in a mesh: section: 8 (over x, core), expert: 32 (over y, z).
Axes of the slice: x: 4, y: 4, z: 8, core: 2. Of those that a mesh axis runs over, the one named last changes fastest.
Arguments:
- layer_inputs: bfloat16 [8, 4, 1024, 2048], P('section', None, 'expert'), may hold values from -6 to 6
- expert_ids: int32 [8, 4, 1024, 3], P('section', None, 'expert'), may hold values from 0 to 31, all different within a row; in each aligned block of 32 rows (0 to 31, 32 to 63, ..., all dimensions but the last counted through in order) at most 4 rows name the same one
- gate_weights: float32 [8, 4, 1024, 3], P('section', None, 'expert'), may hold values from 0.1 to 0.6
- norm_gain: float32 [8, 2048], P('section'), may hold values from 0.1 to 1.9
- w_gate: bfloat16 [8, 32, 2048, 256], P('section', 'expert'), may hold values from -0.125 to 0.125
- w_up: bfloat16 [8, 32, 2048, 256], P('section', 'expert'), may hold values from -0.125 to 0.125
- w_down: bfloat16 [8, 32, 256, 2048], P('section', 'expert'), may hold values from -0.375 to 0.375
- top_cotangent: bfloat16 [4, 1024, 2048], P(None, 'expert'), may hold values from -6 to 6
Outputs:
- input_grads: bfloat16 [8, 4, 1024, 2048], P('section', None, 'expert')
- grad_gate: bfloat16 [8, 32, 2048, 256], P('section', 'expert')
- grad_up: bfloat16 [8, 32, 2048, 256], P('section', 'expert')
- grad_down: bfloat16 [8, 32, 256, 2048], P('section', 'expert')
- gain_grads: float32 [8, 2048], P('section')
The draws below stay inside these ranges and needn't reach their ends.
Inputs may be any that keep to these rules, and one draw needn't show every extreme that they name: `expert_ids`: each token names 3 different experts. Within the 32 tokens of one layer, one micro-batch and one index of expert, no expert is named by more than 4 tokens, a bound that some block reaches.
All inputs are finite; a program needn't handle non-finite values.
Results may differ from the reference program's by a relative error of at most 0.03.
Values may be sent and summed in bfloat16 or wider, within the bound.
A program may use at most 64 MiB of HBM per device.

```python
import math
import jax
import jax.numpy as jnp
import numpy as np
from jax import lax

D = 2048
H = 256
TOP = 3
MB = 4
TOK_MB = 32
LAYERS = 8
EXPERTS = 32
TOKENS = 1024
CAP = 4
N_EXPERT = 32


def block_levels(stream_key, shape, split, smallest, largest):
    level = 1.0
    for axis_at, shards_of in split:
        draws = jax.random.uniform(jax.random.fold_in(jax.random.fold_in(stream_key, 6), axis_at), (shards_of,), jnp.float32, smallest / len(split), largest / len(split))
        level = level * jnp.repeat(jnp.exp(draws), shape[axis_at] // shards_of).reshape((-1,) + (1,) * (len(shape) - 1 - axis_at))
    return level


def routed_block(rng, own, number, rows, count, top, reach, skew):
    ranking = jax.random.permutation(rng, count)
    crowded, usual = shares(count, rows * top, reach, skew, True), shares(count, rows * top, reach, skew, False)
    places = jnp.arange(count)

    def named(sizes, rotation):
        used = int((sizes > 0).sum())
        fixed = max(1, used // 4)
        shifted = fixed + (places - fixed + rotation * (used - fixed)) % max(1, count - fixed)
        return jnp.zeros((count,), jnp.int32).at[ranking[jnp.where(places < fixed, places, shifted)]].set(jnp.asarray(sizes, jnp.int32))

    sizes = jnp.where(number % 4 == 0, named(crowded, number // 4), named(usual, number - number // 4 - 1))
    mixed = jax.random.permutation(jax.random.fold_in(own, 3), count)
    donor, receiver = mixed[0:count // 2 * 2:2], mixed[1:count // 2 * 2:2]
    room = jnp.minimum(sizes[donor] - 1, reach - sizes[receiver]) // 2
    room = jnp.where((donor == ranking[0]) | (receiver == ranking[0]) | (sizes[receiver] == 0), 0, jnp.maximum(room, 0))
    shifted = jax.random.randint(jax.random.fold_in(own, 4), (count // 2,), 0, 1 << 20) % (room + 1)
    sizes = sizes.at[donor].add(-shifted).at[receiver].add(shifted)
    labels = jnp.searchsorted(jnp.cumsum(sizes), jnp.arange(rows * top), side="right").astype(jnp.int32)
    table = labels.reshape(top, rows).T
    table = table[jax.random.permutation(jax.random.fold_in(own, 1), rows)]
    rotation = jax.random.randint(jax.random.fold_in(own, 2), (rows, 1), 0, top)
    return jnp.take_along_axis(table, (jnp.arange(top)[None, :] + rotation) % top, axis=1)


def shares(number_of, total, reach, slope, full):
    loads = [(1 << 20) // math.isqrt(grade ** slope) + 1 for grade in range(1, number_of + 1)]
    largest = reach if full else min(reach, max(-(-total // number_of), total * loads[0] // sum(loads)))
    least = 1 if total - largest >= number_of - 1 else 0
    given, spare = [largest] + [least] * (number_of - 1), total - largest - least * (number_of - 1)
    while spare > 0:
        movable = [i for i in range(1, number_of) if given[i] < largest] or [i for i in range(1, number_of) if given[i] < reach]
        pool, left = sum([loads[i] for i in movable]), spare
        for i in movable:
            extra = min(reach - given[i], max(1, left * loads[i] // pool), spare)
            given[i] = given[i] + extra
            spare = spare - extra
    return np.array(given)


def scatter_about(own_key, extent, scale, limit, split=(), held_as=jnp.bfloat16):
    level = block_levels(own_key, extent, split, -0.22, 0.18) if split else 1.0
    values = jax.random.normal(own_key, extent, jnp.float32) * scale * level
    return jnp.minimum(jnp.maximum(values, -limit), limit).astype(held_as)


def setup_inputs(seed: int = 0) -> dict:
    arg_keys = jax.random.split(jax.random.key(seed), 9)
    layer_inputs = scatter_about(arg_keys[0], (LAYERS, MB, TOKENS, D), 1.0, 6.0, ((0, 8), (2, 32)))
    expert_ids_keys = jax.random.split(jax.random.fold_in(arg_keys[1], 1), LAYERS * MB * TOKENS // TOK_MB)
    expert_ids_turns = jax.random.permutation(jax.random.fold_in(arg_keys[1], 3), LAYERS * MB * TOKENS // TOK_MB)
    expert_ids = jax.vmap(lambda own, number: routed_block(jax.random.fold_in(arg_keys[1], 2), own, number, TOK_MB, EXPERTS, TOP, CAP, 1))(expert_ids_keys, expert_ids_turns).reshape((LAYERS, MB, TOKENS, TOP))
    gate_weights = jnp.clip(0.1 + 0.5 * jax.random.uniform(arg_keys[2], (LAYERS, MB, TOKENS, TOP), jnp.float32) ** block_levels(arg_keys[2], (LAYERS, MB, TOKENS, TOP), ((0, 8), (2, 32)), -0.2, 0.2), 0.1, 0.6)
    norm_gain = jnp.clip(1.0 + 0.18 * jax.random.normal(arg_keys[3], (LAYERS, D), jnp.float32), 0.1, 1.9)
    w_gate = scatter_about(arg_keys[4], (LAYERS, EXPERTS, D, H), D ** -0.5, 0.125, ((0, 8), (1, 32)))
    w_up = scatter_about(arg_keys[5], (LAYERS, EXPERTS, D, H), D ** -0.5, 0.125, ((0, 8), (1, 32)))
    w_down = scatter_about(arg_keys[6], (LAYERS, EXPERTS, H, D), H ** -0.5, 0.375, ((0, 8), (1, 32)))
    top_cotangent = scatter_about(arg_keys[7], (MB, TOKENS, D), 1.0, 6.0, ((1, 32),))
    return {"layer_inputs": layer_inputs, "expert_ids": expert_ids, "gate_weights": gate_weights, "norm_gain": norm_gain, "w_gate": w_gate, "w_up": w_up, "w_down": w_down, "top_cotangent": top_cotangent}


epsilon = 1e-06

def reference(layer_inputs, expert_ids, gate_weights, norm_gain, w_gate, w_up, w_down, top_cotangent):
    cotangents = top_cotangent
    input_list = [None] * LAYERS
    gate_list = [None] * LAYERS
    up_list = [None] * LAYERS
    down_list = [None] * LAYERS
    gain_list = [None] * LAYERS
    for layer in reversed(range(LAYERS)):
        gate_mats = w_gate[layer].astype(jnp.float32)
        up_mats = w_up[layer].astype(jnp.float32)
        down_mats = w_down[layer].astype(jnp.float32)
        acc_gate = jnp.zeros((EXPERTS, D, H), jnp.float32)
        acc_up = jnp.zeros((EXPERTS, D, H), jnp.float32)
        acc_down = jnp.zeros((EXPERTS, H, D), jnp.float32)
        acc_gain = jnp.zeros((D,), jnp.float32)
        produced = []
        for micro in range(MB):
            cotangent = cotangents[micro]
            values = layer_inputs[layer, micro].astype(jnp.float32)
            scales = jax.lax.rsqrt(lax.optimization_barrier(jnp.mean(values * values, axis=-1, keepdims=True)) + epsilon)
            unit_rows = values * scales
            normed = (unit_rows * norm_gain[layer]).astype(jnp.bfloat16)
            blocks = expert_ids[layer, micro].reshape(N_EXPERT, TOK_MB * TOP)
            one_hot = (blocks[:, :, None] == jnp.arange(EXPERTS, dtype=jnp.int32)[None, None, :]).astype(jnp.int32)
            earlier = jnp.cumsum(one_hot, axis=1) - one_hot
            slot_index = lax.optimization_barrier(jnp.sum(earlier * one_hot, axis=-1)).astype(jnp.int32)
            positions = (jnp.arange(N_EXPERT, dtype=jnp.int32)[:, None] * CAP + slot_index).reshape(-1).astype(jnp.int32)
            flat_ids = blocks.reshape(-1).astype(jnp.int32)
            input_rows = jnp.repeat(normed, TOP, axis=0)
            scaled = (gate_weights[layer, micro][:, :, None] * cotangent.astype(jnp.float32)[:, None, :]).astype(jnp.bfloat16)
            scaled = scaled.reshape(-1, D)
            buffer_in = jnp.zeros((EXPERTS, N_EXPERT * CAP, D), jnp.bfloat16).at[flat_ids, positions].set(input_rows)
            buffer_cot = jnp.zeros((EXPERTS, N_EXPERT * CAP, D), jnp.bfloat16).at[flat_ids, positions].set(scaled)
            inputs_wide = buffer_in.astype(jnp.float32)
            cot_wide = buffer_cot.astype(jnp.float32)
            pre_gate = jnp.einsum('erd,edh->erh', inputs_wide, gate_mats)
            pre_up = jnp.einsum('erd,edh->erh', inputs_wide, up_mats)
            sigma = jax.nn.sigmoid(pre_gate)
            silu_gate = pre_gate * sigma
            activated = (silu_gate * pre_up).astype(jnp.bfloat16)
            d_act = jnp.einsum('erd,ehd->erh', cot_wide, down_mats)
            d_gate = (d_act * pre_up * sigma * (1.0 + pre_gate * (1.0 - sigma))).astype(jnp.bfloat16)
            d_up = (d_act * silu_gate).astype(jnp.bfloat16)
            returned = (jnp.einsum('erh,edh->erd', d_gate.astype(jnp.float32), gate_mats) + jnp.einsum('erh,edh->erd', d_up.astype(jnp.float32), up_mats)).astype(jnp.bfloat16)
            acc_gate = acc_gate + jnp.einsum('erd,erh->edh', inputs_wide, d_gate.astype(jnp.float32))
            acc_up = acc_up + jnp.einsum('erd,erh->edh', inputs_wide, d_up.astype(jnp.float32))
            acc_down = acc_down + jnp.einsum('erh,erd->ehd', activated.astype(jnp.float32), cot_wide)
            row_grads = returned[flat_ids, positions].astype(jnp.float32)
            d_normed = lax.optimization_barrier(jnp.sum(row_grads.reshape(TOKENS, TOP, D), axis=1))
            acc_gain = acc_gain + lax.optimization_barrier(jnp.sum(d_normed * unit_rows, axis=0))
            scaled_grad = d_normed * norm_gain[layer]
            input_grad = cotangent.astype(jnp.float32) + scales * (scaled_grad - unit_rows * lax.optimization_barrier(jnp.mean(scaled_grad * unit_rows, axis=-1, keepdims=True)))
            produced.append(input_grad.astype(jnp.bfloat16))
        cotangents = jnp.stack(produced)
        input_list[layer] = cotangents
        gate_list[layer] = acc_gate.astype(jnp.bfloat16)
        up_list[layer] = acc_up.astype(jnp.bfloat16)
        down_list[layer] = acc_down.astype(jnp.bfloat16)
        gain_list[layer] = acc_gain
    return (jnp.stack(input_list), jnp.stack(gate_list), jnp.stack(up_list), jnp.stack(down_list), jnp.stack(gain_list))
```

```python
import functools

import jax
import jax.numpy as jnp
from jax import lax
from jax.experimental import pallas as pl
from jax.experimental.pallas import tpu as pltpu
from jax.sharding import PartitionSpec as P

epsilon = 1e-06
MESH = pl.DeviceIdType.MESH
F32 = jnp.float32
BF16 = jnp.bfloat16

SECTIONS = 8
NY, NZ = 4, 8
EXPERTS = NY * NZ
MICRO = 4
ROWS = 32
TOP = 3
WIDTH = 2048
HALF = WIDTH // 2
HIDDEN = 256
CAP = 4
BLOCK = 2 * CAP
SLOTS = EXPERTS * BLOCK


def dot(left, right, left_dim=1, right_dim=0):
    return lax.dot_general(
        left, right, (((left_dim,), (right_dim,)), ((), ())), preferred_element_type=F32
    )


def peer(step, index):
    y, z = index // NZ, index % NZ
    across, along = step // NY, step % NY
    dz = NZ // 2 + ((across + 1) // 2) * (1 - 2 * (across % 2))
    dy = NY // 2 + ((along + 1) // 2) * (1 - 2 * (along % 2))
    return ((y + dy) % NY) * NZ + (z + dz + NZ) % NZ


def routing(ids, weights):
    lane = lax.broadcasted_iota(jnp.int32, (ROWS, SLOTS), 1)
    expert = (lane // BLOCK).astype(F32)
    named = jnp.zeros((ROWS, SLOTS), F32)
    weight = jnp.zeros((ROWS, SLOTS), F32)
    for k in range(TOP):
        hit = ids[:, k : k + 1] == expert
        named = named + jnp.where(hit, 1.0, 0.0)
        weight = weight + jnp.where(hit, weights[:, k : k + 1], 0.0)
    before = (
        lax.broadcasted_iota(jnp.int32, (ROWS, ROWS), 1)
        < lax.broadcasted_iota(jnp.int32, (ROWS, ROWS), 0)
    ).astype(F32)
    earlier = dot(before.astype(BF16), named.astype(BF16))
    placed = jnp.where(earlier == (lane % CAP).astype(F32), named, 0.0)
    first = (lane % BLOCK) < CAP
    from_slots = jnp.concatenate(
        [jnp.where(first, placed, 0.0), jnp.where(first, 0.0, placed)], axis=0
    )
    slot_weight = jnp.sum(placed * weight, axis=0, keepdims=True)
    both = jnp.concatenate(
        [from_slots, jnp.broadcast_to(slot_weight, (128 - 2 * ROWS, SLOTS))], axis=0
    )
    turned = both.T
    to_slots = turned[:, : 2 * ROWS].astype(BF16)
    slot_weights = jnp.broadcast_to(turned[:, 2 * ROWS : 2 * ROWS + 1], (SLOTS, 128))
    return to_slots, from_slots.astype(BF16), slot_weights


def halves(value):
    return jnp.concatenate([value[:, :HALF], value[:, HALF:]], axis=0)


def first_rows(shape):
    return (lax.broadcasted_iota(jnp.int32, shape, 0) % BLOCK) < CAP


def by_half(first, second):
    own = jnp.where(first_rows(first.shape), first, second)
    grouped = own.reshape(EXPERTS, BLOCK, own.shape[-1])
    return (grouped + pltpu.roll(grouped, CAP, 1)).reshape(own.shape)


def scale_rows(rows, slot_weights):
    return rows * jnp.concatenate([slot_weights] * (rows.shape[1] // 128), axis=1)


def kernel(
    inputs_ref,
    ids_ref,
    gates_ref,
    gain_ref,
    top_ref,
    w_gate_hbm,
    w_up_hbm,
    w_down_hbm,
    out_ref,
    grad_gate_ref,
    grad_up_ref,
    grad_down_ref,
    gain_out_ref,
    w_gate,
    w_up,
    w_down,
    meta_own,
    meta_next,
    own_to,
    own_from,
    own_weight,
    next_to,
    next_weight,
    unit,
    scale,
    cot,
    cot_out,
    in_send,
    in_recv,
    top_send,
    cot_send,
    cot_recv,
    ret_send,
    ret_recv,
    coef_gate,
    coef_up,
    act,
    d_gate_rows,
    d_up_rows,
    acc_gate,
    acc_up,
    acc_down,
    gain_part,
    gain_all,
    load_sem,
    meta_send_sem,
    meta_recv_sem,
    in_send_sem,
    in_recv_sem,
    top_send_sem,
    cot_send_sem,
    cot_recv_sem,
    res_send_sem,
    res_recv_sem,
    ret_send_sem,
    ret_recv_sem,
    gain_send_sem,
    gain_recv_sem,
):
    section = lax.axis_index("section")
    index = lax.axis_index("expert")
    is_top = section == SECTIONS - 1
    is_last = section == 0

    loads = [
        pltpu.make_async_copy(source, target, load_sem.at[number])
        for number, (source, target) in enumerate(
            [(w_gate_hbm, w_gate), (w_up_hbm, w_up), (w_down_hbm, w_down)]
        )
    ]
    for load in loads:
        load.start()

    barrier = pltpu.get_barrier_semaphore()

    def greet(to_section, count):
        def step(number, carry):
            pl.semaphore_signal(
                barrier, inc=1, device_id=(to_section, peer(number, index)), device_id_type=MESH
            )
            return carry

        lax.fori_loop(0, count, step, 0)

    greet(section, EXPERTS - 1)

    @pl.when(jnp.logical_not(is_top))
    def _():
        greet(section + 1, EXPERTS)

    @pl.when(jnp.logical_not(is_last))
    def _():
        pl.semaphore_signal(
            barrier, inc=1, device_id=(section - 1, index), device_id_type=MESH
        )

    def send_blocks(source, target, m, to_section, send_sem, recv_sem, count):
        def step(number, carry):
            to = peer(number, index)
            pltpu.make_async_remote_copy(
                source.at[m, to],
                target.at[m, index],
                send_sem.at[m],
                recv_sem.at[m],
                device_id=(to_section, to),
                device_id_type=MESH,
            ).start()
            return carry

        lax.fori_loop(0, count, step, 0)

    def keep_own(source, target, m, recv_sem):
        pltpu.make_async_copy(
            source.at[m, index], target.at[m, index], recv_sem.at[m]
        ).start()

    def wait_blocks(ref, m, sem, count):
        part = ref.at[m, pl.ds(0, count)]
        pltpu.make_async_copy(part, part, sem.at[m]).wait()

    def prepare(m):
        values = inputs_ref[0, m].astype(F32)
        scales = lax.rsqrt(jnp.mean(values * values, axis=-1, keepdims=True) + epsilon)
        unit_rows = values * scales
        normed = (unit_rows * gain_ref[...]).astype(BF16)
        unit[m] = halves(unit_rows)
        scale[m] = jnp.broadcast_to(scales, (ROWS, 128))
        ids = ids_ref[0, m].astype(F32)
        weights = gates_ref[0, m]
        to_slots, from_slots, slot_weights = routing(ids, weights)
        own_to[m] = to_slots
        own_from[m] = from_slots
        own_weight[m] = slot_weights
        meta_own[m] = jnp.concatenate(
            [ids, weights, jnp.zeros((ROWS, 128 - 2 * TOP), F32)], axis=1
        )
        in_send[m] = dot(to_slots, halves(normed)).astype(BF16).reshape(EXPERTS, BLOCK, HALF)

        @pl.when(is_top)
        def _():
            rows = halves(top_ref[m])
            cot[m] = rows
            top_send[m] = (
                scale_rows(dot(to_slots, rows), slot_weights)
                .astype(BF16)
                .reshape(EXPERTS, BLOCK, HALF)
            )

    def send_inputs(m):
        send_blocks(in_send, in_recv, m, section, in_send_sem, in_recv_sem, EXPERTS - 1)
        keep_own(in_send, in_recv, m, in_recv_sem)

    def send_top(m):
        send_blocks(top_send, cot_recv, m, section, top_send_sem, cot_recv_sem, EXPERTS - 1)
        keep_own(top_send, cot_recv, m, cot_recv_sem)

    prepare(0)
    pl.semaphore_wait(
        barrier,
        EXPERTS - 1
        + jnp.where(is_last, 0, EXPERTS)
        + jnp.where(is_top, 0, 1),
    )
    send_inputs(0)
    pl.when(is_top)(lambda: send_top(0))

    def prepare_rest(m, carry):
        prepare(m)

        @pl.when(jnp.logical_not(is_top))
        def _():
            send_inputs(m)

        return carry

    lax.fori_loop(1, MICRO, prepare_rest, 0)

    @pl.when(jnp.logical_not(is_top))
    def _():
        pltpu.make_async_remote_copy(
            meta_own,
            meta_next,
            meta_send_sem,
            meta_recv_sem,
            device_id=(section + 1, index),
            device_id_type=MESH,
        ).start()

    acc_gate[...] = jnp.zeros_like(acc_gate)
    acc_up[...] = jnp.zeros_like(acc_up)
    acc_down[...] = jnp.zeros_like(acc_down)
    gain_part[...] = jnp.zeros_like(gain_part)

    @pl.when(jnp.logical_not(is_last))
    def _():
        pltpu.make_async_copy(meta_next, meta_next, meta_recv_sem).wait()

        def step(m, carry):
            known = meta_next[m]
            to_slots, _, slot_weights = routing(known[:, :TOP], known[:, TOP : 2 * TOP])
            next_to[m] = to_slots
            next_weight[m] = slot_weights
            return carry

        lax.fori_loop(0, MICRO, step, 0)

    for load in loads:
        load.wait()

    def before(m):
        wait_blocks(in_recv, m, in_recv_sem, EXPERTS)
        rows = in_recv[m].reshape(SLOTS, HALF)
        pre_gate = by_half(dot(rows, w_gate[:HALF]), dot(rows, w_gate[HALF:]))
        pre_up = by_half(dot(rows, w_up[:HALF]), dot(rows, w_up[HALF:]))
        sigma = jax.nn.sigmoid(pre_gate)
        silu = pre_gate * sigma
        act[m] = (silu * pre_up).astype(BF16)
        coef_gate[m] = pre_up * sigma * (1.0 + pre_gate * (1.0 - sigma))
        coef_up[m] = silu

    before(0)

    def one_micro(m, carry):
        wait_blocks(cot_recv, m, cot_recv_sem, EXPERTS)
        rows = cot_recv[m].reshape(SLOTS, HALF)
        d_act = by_half(
            dot(rows, w_down[:, :HALF], 1, 1), dot(rows, w_down[:, HALF:], 1, 1)
        )
        d_gate = (d_act * coef_gate[m]).astype(BF16)
        d_up = (d_act * coef_up[m]).astype(BF16)
        d_gate_rows[...] = d_gate
        d_up_rows[...] = d_up
        low = dot(d_gate, w_gate[:HALF], 1, 1) + dot(d_up, w_up[:HALF], 1, 1)
        high = dot(d_gate, w_gate[HALF:], 1, 1) + dot(d_up, w_up[HALF:], 1, 1)
        ret_send[m] = (
            jnp.where(first_rows(low.shape), low, high)
            .astype(BF16)
            .reshape(EXPERTS, BLOCK, HALF)
        )
        send_blocks(ret_send, ret_recv, m, section, ret_send_sem, ret_recv_sem, EXPERTS - 1)
        keep_own(ret_send, ret_recv, m, ret_recv_sem)

        if m < MICRO - 1:

            @pl.when(is_top)
            def _():
                send_inputs(m + 1)
                send_top(m + 1)

        in_rows = in_recv[m].reshape(SLOTS, HALF)
        cot_rows = cot_recv[m].reshape(SLOTS, HALF)
        left = (lax.broadcasted_iota(jnp.int32, (HIDDEN, SLOTS), 1) % BLOCK) < CAP
        for rows_ref, total, others in (
            (d_gate_rows[...], acc_gate, in_rows),
            (d_up_rows[...], acc_up, in_rows),
            (act[m], acc_down, cot_rows),
        ):
            turned = rows_ref.astype(F32).T
            total[0] += dot(jnp.where(left, turned, 0.0).astype(BF16), others)
            total[1] += dot(jnp.where(left, 0.0, turned).astype(BF16), others)

        if m < MICRO - 1:
            before(m + 1)
        else:
            for half in range(2):
                span = pl.ds(half * HALF, HALF)
                grad_gate_ref[span, :] = acc_gate[half].T.astype(BF16)
                grad_up_ref[span, :] = acc_up[half].T.astype(BF16)
                grad_down_ref[:, span] = acc_down[half].astype(BF16)

        @pl.when(jnp.logical_not(is_top))
        def _():
            pltpu.make_async_copy(cot.at[m], cot.at[m], res_recv_sem.at[m]).wait()

        wait_blocks(ret_recv, m, ret_recv_sem, EXPERTS)
        d_normed = dot(own_from[m], ret_recv[m].reshape(SLOTS, HALF))
        units = unit[m]
        gained = d_normed * units
        gain_part[...] += jnp.concatenate(
            [
                jnp.sum(gained[:ROWS], axis=0, keepdims=True),
                jnp.sum(gained[ROWS:], axis=0, keepdims=True),
            ],
            axis=0,
        )
        gain = jnp.concatenate(
            [
                jnp.broadcast_to(gain_ref[:, :HALF], (ROWS, HALF)),
                jnp.broadcast_to(gain_ref[:, HALF:], (ROWS, HALF)),
            ],
            axis=0,
        )
        scaled = d_normed * gain
        sums = jnp.sum(scaled * units, axis=-1, keepdims=True)
        mean = (sums[:ROWS] + sums[ROWS:]) * (1.0 / WIDTH)
        means = jnp.concatenate([mean, mean], axis=0)
        scales = scale[m][:, :1]
        scales = jnp.concatenate([scales, scales], axis=0)
        grad = (cot[m].astype(F32) + scales * (scaled - units * means)).astype(BF16)
        out_ref[0, m, :, :HALF] = grad[:ROWS]
        out_ref[0, m, :, HALF:] = grad[ROWS:]

        @pl.when(jnp.logical_not(is_last))
        def _():
            cot_send[m] = (
                scale_rows(dot(next_to[m], grad), next_weight[m])
                .astype(BF16)
                .reshape(EXPERTS, BLOCK, HALF)
            )
            cot_out[m] = grad
            send_blocks(
                cot_send, cot_recv, m, section - 1, cot_send_sem, cot_recv_sem, EXPERTS
            )
            pltpu.make_async_remote_copy(
                cot_out.at[m],
                cot.at[m],
                res_send_sem.at[m],
                res_recv_sem.at[m],
                device_id=(section - 1, index),
                device_id_type=MESH,
            ).start()

        return carry

    for m in range(MICRO):
        one_micro(m, 0)

    gain_all[index] = gain_part[...]

    def send_gain(number, carry):
        pltpu.make_async_remote_copy(
            gain_part,
            gain_all.at[index],
            gain_send_sem,
            gain_recv_sem,
            device_id=(section, peer(number, index)),
            device_id_type=MESH,
        ).start()
        return carry

    lax.fori_loop(0, EXPERTS - 1, send_gain, 0)

    def drain(m, carry):
        wait_blocks(in_send, m, in_send_sem, EXPERTS - 1)
        wait_blocks(ret_send, m, ret_send_sem, EXPERTS - 1)

        @pl.when(is_top)
        def _():
            wait_blocks(top_send, m, top_send_sem, EXPERTS - 1)

        @pl.when(jnp.logical_not(is_last))
        def _():
            wait_blocks(cot_send, m, cot_send_sem, EXPERTS)
            pltpu.make_async_copy(cot_out.at[m], cot_out.at[m], res_send_sem.at[m]).wait()

        return carry

    lax.fori_loop(0, MICRO, drain, 0)

    @pl.when(jnp.logical_not(is_top))
    def _():
        pltpu.make_async_copy(meta_own, meta_own, meta_send_sem).wait()

    others = gain_all.at[pl.ds(0, EXPERTS - 1)]
    pltpu.make_async_copy(others, others, gain_recv_sem).wait()
    pltpu.make_async_copy(others, others, gain_send_sem).wait()
    total = jnp.sum(gain_all[...], axis=0)
    gain_out_ref[:, :HALF] = total[:1]
    gain_out_ref[:, HALF:] = total[1:]


def local(layer_inputs, expert_ids, gate_weights, norm_gain, w_gate, w_up, w_down, top_cotangent):
    blocks = pltpu.VMEM((MICRO, EXPERTS, BLOCK, HALF), BF16)
    vmem = pl.BlockSpec(memory_space=pltpu.VMEM)
    hbm = pl.BlockSpec(memory_space=pl.ANY)
    dma = pltpu.SemaphoreType.DMA
    outs = pl.pallas_call(
        kernel,
        out_shape=(
            jax.ShapeDtypeStruct((1, MICRO, ROWS, WIDTH), BF16),
            jax.ShapeDtypeStruct((WIDTH, HIDDEN), BF16),
            jax.ShapeDtypeStruct((WIDTH, HIDDEN), BF16),
            jax.ShapeDtypeStruct((HIDDEN, WIDTH), BF16),
            jax.ShapeDtypeStruct((1, WIDTH), F32),
        ),
        in_specs=[vmem] * 5 + [hbm] * 3,
        out_specs=(vmem,) * 5,
        scratch_shapes=[
            pltpu.VMEM((WIDTH, HIDDEN), BF16),
            pltpu.VMEM((WIDTH, HIDDEN), BF16),
            pltpu.VMEM((HIDDEN, WIDTH), BF16),
            pltpu.VMEM((MICRO, ROWS, 128), F32),
            pltpu.VMEM((MICRO, ROWS, 128), F32),
            pltpu.VMEM((MICRO, SLOTS, 2 * ROWS), BF16),
            pltpu.VMEM((MICRO, 2 * ROWS, SLOTS), BF16),
            pltpu.VMEM((MICRO, SLOTS, 128), F32),
            pltpu.VMEM((MICRO, SLOTS, 2 * ROWS), BF16),
            pltpu.VMEM((MICRO, SLOTS, 128), F32),
            pltpu.VMEM((MICRO, 2 * ROWS, HALF), F32),
            pltpu.VMEM((MICRO, ROWS, 128), F32),
            pltpu.VMEM((MICRO, 2 * ROWS, HALF), BF16),
            pltpu.VMEM((MICRO, 2 * ROWS, HALF), BF16),
            blocks,
            blocks,
            blocks,
            blocks,
            blocks,
            blocks,
            blocks,
            pltpu.VMEM((MICRO, SLOTS, HIDDEN), F32),
            pltpu.VMEM((MICRO, SLOTS, HIDDEN), F32),
            pltpu.VMEM((MICRO, SLOTS, HIDDEN), BF16),
            pltpu.VMEM((SLOTS, HIDDEN), BF16),
            pltpu.VMEM((SLOTS, HIDDEN), BF16),
            pltpu.VMEM((2, HIDDEN, HALF), F32),
            pltpu.VMEM((2, HIDDEN, HALF), F32),
            pltpu.VMEM((2, HIDDEN, HALF), F32),
            pltpu.VMEM((2, HALF), F32),
            pltpu.VMEM((EXPERTS, 2, HALF), F32),
            dma((3,)),
            dma,
            dma,
            dma((MICRO,)),
            dma((MICRO,)),
            dma((MICRO,)),
            dma((MICRO,)),
            dma((MICRO,)),
            dma((MICRO,)),
            dma((MICRO,)),
            dma((MICRO,)),
            dma((MICRO,)),
            dma,
            dma,
        ],
        compiler_params=pltpu.CompilerParams(
            collective_id=0, has_side_effects=True, vmem_limit_bytes=56 * 1024 * 1024
        ),
    )(
        layer_inputs,
        expert_ids,
        gate_weights,
        norm_gain,
        top_cotangent,
        w_gate[0, 0],
        w_up[0, 0],
        w_down[0, 0],
    )
    return (outs[0], outs[1][None, None], outs[2][None, None], outs[3][None, None], outs[4])


def solution(mesh):
    in_specs = (
        P("section", None, "expert", None),
        P("section", None, "expert", None),
        P("section", None, "expert", None),
        P("section", None),
        P("section", "expert", None, None),
        P("section", "expert", None, None),
        P("section", "expert", None, None),
        P(None, "expert", None),
    )
    out_specs = (
        P("section", None, "expert", None),
        P("section", "expert", None, None),
        P("section", "expert", None, None),
        P("section", "expert", None, None),
        P("section", None),
    )
    return jax.shard_map(local, mesh=mesh, in_specs=in_specs, out_specs=out_specs, check_vma=False)
```

```python
import functools

import jax
import jax.numpy as jnp
from jax import lax
from jax.experimental import pallas as pl
from jax.experimental.pallas import tpu as pltpu
from jax.sharding import PartitionSpec as P

epsilon = 1e-06
MESH = pl.DeviceIdType.MESH
F32 = jnp.float32
BF16 = jnp.bfloat16

SECTIONS = 8
NY, NZ = 4, 8
EXPERTS = NY * NZ
MICRO = 4
ROWS = 32
TOP = 3
WIDTH = 2048
HALF = WIDTH // 2
HIDDEN = 256
CAP = 4
BLOCK = 2 * CAP
SLOTS = EXPERTS * BLOCK
PART = EXPERTS // 2


def dot(left, right, left_dim=1, right_dim=0):
    return lax.dot_general(
        left, right, (((left_dim,), (right_dim,)), ((), ())), preferred_element_type=F32
    )


def offsets(step):
    across, along = step // NY, step % NY
    dz = NZ // 2 + ((across + 1) // 2) * (1 - 2 * (across % 2))
    dy = NY // 2 + ((along + 1) // 2) * (1 - 2 * (along % 2))
    return dy % NY, dz % NZ


def peer(step, index):
    dy, dz = offsets(step)
    return ((index // NZ + dy) % NY) * NZ + (index % NZ + dz) % NZ


def source(step, index):
    dy, dz = offsets(step)
    return ((index // NZ - dy + NY) % NY) * NZ + (index % NZ - dz + NZ) % NZ


def routing(known, index):
    columns = known.T[:ROWS]
    lane = lax.broadcasted_iota(jnp.int32, (ROWS, SLOTS), 1)
    expert = peer(lane // BLOCK, index).astype(F32)
    named = jnp.zeros((ROWS, SLOTS), F32)
    weight = jnp.zeros((ROWS, SLOTS), F32)
    for k in range(TOP):
        hit = columns[:, k : k + 1] == expert
        named = named + jnp.where(hit, 1.0, 0.0)
        weight = weight + jnp.where(hit, columns[:, TOP + k : TOP + k + 1], 0.0)
    before = (
        lax.broadcasted_iota(jnp.int32, (ROWS, ROWS), 1)
        < lax.broadcasted_iota(jnp.int32, (ROWS, ROWS), 0)
    ).astype(F32)
    earlier = dot(before.astype(BF16), named.astype(BF16))
    placed = jnp.where(earlier == (lane % CAP).astype(F32), named, 0.0)
    first = (lane % BLOCK) < CAP
    from_slots = jnp.concatenate(
        [jnp.where(first, placed, 0.0), jnp.where(first, 0.0, placed)], axis=0
    )
    slot_weight = jnp.sum(placed * weight, axis=0, keepdims=True)
    both = jnp.concatenate(
        [from_slots, jnp.broadcast_to(slot_weight, (128 - 2 * ROWS, SLOTS))], axis=0
    )
    turned = both.T
    to_slots = turned[:, : 2 * ROWS].astype(BF16)
    slot_weights = jnp.broadcast_to(turned[:, 2 * ROWS : 2 * ROWS + 1], (SLOTS, 128))
    return to_slots, from_slots.astype(BF16), slot_weights


def halves(value):
    return jnp.concatenate([value[:, :HALF], value[:, HALF:]], axis=0)


def first_rows(shape):
    return (lax.broadcasted_iota(jnp.int32, shape, 0) % BLOCK) < CAP


def by_half(first, second):
    own = jnp.where(first_rows(first.shape), first, second)
    grouped = own.reshape(own.shape[0] // BLOCK, BLOCK, own.shape[-1])
    return (grouped + pltpu.roll(grouped, CAP, 1)).reshape(own.shape)


def scale_rows(rows, slot_weights):
    return rows * jnp.concatenate([slot_weights] * (rows.shape[1] // 128), axis=1)


def kernel(
    inputs_ref,
    ids_ref,
    gates_ref,
    gain_ref,
    top_ref,
    w_gate_hbm,
    w_up_hbm,
    w_down_hbm,
    out_ref,
    grad_gate_ref,
    grad_up_ref,
    grad_down_ref,
    gain_out_ref,
    w_gate,
    w_up,
    w_down,
    meta_own,
    meta_next,
    meta_help,
    own_to,
    own_from,
    own_weight,
    next_to,
    next_weight,
    unit,
    scale,
    cot,
    cot_out,
    normed,
    help_rows,
    in_send,
    in_recv,
    top_send,
    cot_send,
    cot_recv,
    ret_send,
    ret_recv,
    coef_gate,
    coef_up,
    act,
    d_gate_rows,
    d_up_rows,
    acc_gate,
    acc_up,
    acc_down,
    gain_part,
    gain_all,
    load_sem,
    meta_send_sem,
    meta_recv_sem,
    meta_help_send_sem,
    meta_help_recv_sem,
    rows_send_sem,
    rows_recv_sem,
    in_send_sem,
    in_recv_sem,
    top_send_sem,
    cot_send_sem,
    cot_recv_sem,
    res_send_sem,
    res_recv_sem,
    ret_send_sem,
    ret_recv_sem,
    gain_send_sem,
    gain_recv_sem,
):
    section = lax.axis_index("section")
    index = lax.axis_index("expert")
    is_top = section == SECTIONS - 1
    is_last = section == 0

    loads = [
        pltpu.make_async_copy(source, target, load_sem.at[number])
        for number, (source, target) in enumerate(
            [(w_gate_hbm, w_gate), (w_up_hbm, w_up), (w_down_hbm, w_down)]
        )
    ]
    for load in loads:
        load.start()

    barrier = pltpu.get_barrier_semaphore()

    def greet(to_section, count):
        def step(number, carry):
            pl.semaphore_signal(
                barrier, inc=1, device_id=(to_section, peer(number, index)), device_id_type=MESH
            )
            return carry

        lax.fori_loop(0, count, step, 0)

    helps_inputs = section == 1
    helps_top = section == 0
    helps_second = section == 3
    is_helper = helps_inputs | helps_top | helps_second
    is_second = section == SECTIONS - 2

    def hello(to_section):
        pl.semaphore_signal(
            barrier, inc=1, device_id=(to_section, index), device_id_type=MESH
        )

    greet(section, EXPERTS - 1)
    pl.when(jnp.logical_not(is_top))(lambda: greet(section + 1, EXPERTS))
    pl.when(jnp.logical_not(is_last))(lambda: hello(section - 1))
    pl.when(helps_inputs | helps_top)(lambda: hello(SECTIONS - 1))
    pl.when(helps_second)(lambda: hello(SECTIONS - 2))

    def send_blocks(source_ref, target, m, to_section, send_sem, recv_sem, first, last, back=False):
        def step(number, carry):
            to = source(number, index) if back else peer(number, index)
            pltpu.make_async_remote_copy(
                source_ref.at[m, number],
                target.at[m, number],
                send_sem,
                recv_sem,
                device_id=(to_section, to),
                device_id_type=MESH,
            ).start()
            return carry

        lax.fori_loop(first, last, step, 0)

    def keep_own(source_ref, target, m, recv_sem):
        pltpu.make_async_copy(
            source_ref.at[m, EXPERTS - 1], target.at[m, EXPERTS - 1], recv_sem
        ).start()

    def wait_blocks(ref, m, sem, first, count):
        part = ref.at[m, pl.ds(first, count)]
        pltpu.make_async_copy(part, part, sem).wait()

    def send_one(source_ref, target, to_section, send_sem, recv_sem):
        pltpu.make_async_remote_copy(
            source_ref,
            target,
            send_sem,
            recv_sem,
            device_id=(to_section, index),
            device_id_type=MESH,
        ).start()

    meta_own[...] = jnp.zeros_like(meta_own)
    for m in range(MICRO):
        for k in range(TOP):
            meta_own[m, k : k + 1, 0:ROWS] = ids_ref[0, k, m : m + 1].astype(F32)
            meta_own[m, TOP + k : TOP + k + 1, 0:ROWS] = gates_ref[0, k, m : m + 1]

    def prepare(m):
        values = inputs_ref[0, m].astype(F32)
        scales = lax.rsqrt(jnp.mean(values * values, axis=-1, keepdims=True) + epsilon)
        unit_rows = values * scales
        normed[m] = halves((unit_rows * gain_ref[...]).astype(BF16))
        unit[m] = halves(unit_rows)
        scale[m] = jnp.broadcast_to(scales, (ROWS, 128))
        to_slots, from_slots, slot_weights = routing(meta_own[m], index)
        own_to[m] = to_slots
        own_from[m] = from_slots
        own_weight[m] = slot_weights
        pl.when(is_top)(lambda: cot.__setitem__(m, halves(top_ref[m])))

    def spread(placing, rows):
        return dot(placing, rows).astype(BF16).reshape(EXPERTS, BLOCK, HALF)

    def spread_scaled(placing, rows, weights):
        scaled = scale_rows(dot(placing, rows), weights)
        return scaled.astype(BF16).reshape(placing.shape[0] // BLOCK, BLOCK, HALF)

    def send_inputs(m):
        in_send[m] = spread(own_to[m], normed[m])
        send_blocks(
            in_send, in_recv, m, section, in_send_sem.at[m], in_recv_sem.at[m], 0, EXPERTS - 1
        )
        keep_own(in_send, in_recv, m, in_recv_sem.at[m])

    prepare(0)
    pl.semaphore_wait(
        barrier,
        EXPERTS - 1
        + jnp.where(is_last, 0, EXPERTS)
        + jnp.where(is_top, 2, 1)
        + jnp.where(is_helper, EXPERTS, 0)
        + jnp.where(is_second, 1, 0),
    )

    @pl.when(is_top)
    def _():
        send_inputs(0)
        top_send[0] = spread_scaled(own_to[0], cot[0], own_weight[0])
        for part in range(2):
            send_blocks(
                top_send,
                cot_recv,
                0,
                section,
                top_send_sem.at[0],
                cot_recv_sem.at[0, part],
                part * PART,
                PART + part * (PART - 1),
            )
        keep_own(top_send, cot_recv, 0, cot_recv_sem.at[0, 1])
        greet(1, EXPERTS)
        greet(0, EXPERTS)
        send_one(meta_own, meta_help, 1, meta_help_send_sem.at[0], meta_help_recv_sem)
        send_one(meta_own, meta_help, 0, meta_help_send_sem.at[1], meta_help_recv_sem)

    @pl.when(is_second)
    def _():
        greet(3, EXPERTS)
        send_one(meta_own, meta_help, 3, meta_help_send_sem.at[0], meta_help_recv_sem)
        send_one(normed.at[0], help_rows.at[0], 3, rows_send_sem.at[0], rows_recv_sem.at[0])

    pl.when(section < SECTIONS - 2)(lambda: send_inputs(0))

    @pl.when(jnp.logical_not(is_top))
    def _():
        send_one(meta_own, meta_next, section + 1, meta_send_sem, meta_recv_sem)

    def prepare_rest(m, carry):
        prepare(m)

        @pl.when(is_top)
        def _():
            send_one(normed.at[m], help_rows.at[m], 1, rows_send_sem.at[m], rows_recv_sem.at[m])

        @pl.when(is_second)
        def _():
            send_one(normed.at[m], help_rows.at[m], 3, rows_send_sem.at[m], rows_recv_sem.at[m])

        @pl.when((section < SECTIONS - 2) & jnp.logical_not(is_helper))
        def _():
            send_inputs(m)

        return carry

    lax.fori_loop(1, MICRO, prepare_rest, 0)

    @pl.when(is_helper)
    def _():
        pltpu.make_async_copy(meta_help, meta_help, meta_help_recv_sem).wait()

        def help_one(m, carry):
            placing, _, weights = routing(meta_help[m], index)

            @pl.when(helps_top)
            def _():
                top_send[m] = spread_scaled(placing, halves(top_ref[m]), weights)
                for part in range(2):
                    send_blocks(
                        top_send,
                        cot_recv,
                        m,
                        SECTIONS - 1,
                        top_send_sem.at[m],
                        cot_recv_sem.at[m, part],
                        part * PART,
                        PART + part * PART,
                    )

            @pl.when(jnp.logical_not(helps_top))
            def _():
                pltpu.make_async_copy(help_rows.at[m], help_rows.at[m], rows_recv_sem.at[m]).wait()
                top_send[m] = spread(placing, help_rows[m])
                send_blocks(
                    top_send,
                    in_recv,
                    m,
                    jnp.where(helps_second, SECTIONS - 2, SECTIONS - 1),
                    top_send_sem.at[m],
                    in_recv_sem.at[m],
                    0,
                    EXPERTS,
                )

            return carry

        lax.fori_loop(jnp.where(helps_second, 0, 1), MICRO, help_one, 0)

        def own_rest(m, carry):
            send_inputs(m)
            return carry

        lax.fori_loop(1, MICRO, own_rest, 0)

    acc_gate[...] = jnp.zeros_like(acc_gate)
    acc_up[...] = jnp.zeros_like(acc_up)
    acc_down[...] = jnp.zeros_like(acc_down)
    gain_part[...] = jnp.zeros_like(gain_part)

    @pl.when(jnp.logical_not(is_last))
    def _():
        pltpu.make_async_copy(meta_next, meta_next, meta_recv_sem).wait()

        def step(m, carry):
            to_slots, _, slot_weights = routing(meta_next[m], index)
            next_to[m] = to_slots
            next_weight[m] = slot_weights
            return carry

        lax.fori_loop(0, MICRO, step, 0)

    for load in loads:
        load.wait()

    def before(m):
        wait_blocks(in_recv, m, in_recv_sem.at[m], 0, EXPERTS)
        rows = in_recv[m].reshape(SLOTS, HALF)
        pre_gate = by_half(dot(rows, w_gate[:HALF]), dot(rows, w_gate[HALF:]))
        pre_up = by_half(dot(rows, w_up[:HALF]), dot(rows, w_up[HALF:]))
        sigma = jax.nn.sigmoid(pre_gate)
        silu = pre_gate * sigma
        act[m] = (silu * pre_up).astype(BF16)
        coef_gate[m] = pre_up * sigma * (1.0 + pre_gate * (1.0 - sigma))
        coef_up[m] = silu

    before(0)

    def one_micro(m, carry):
        for part in range(2):
            blocks = pl.ds(part * PART, PART)
            span = pl.ds(part * PART * BLOCK, PART * BLOCK)
            wait_blocks(cot_recv, m, cot_recv_sem.at[m, part], part * PART, PART)
            rows = cot_recv[m, blocks].reshape(PART * BLOCK, HALF)
            d_act = by_half(
                dot(rows, w_down[:, :HALF], 1, 1), dot(rows, w_down[:, HALF:], 1, 1)
            )
            d_gate = (d_act * coef_gate[m, span]).astype(BF16)
            d_up = (d_act * coef_up[m, span]).astype(BF16)
            d_gate_rows[span] = d_gate
            d_up_rows[span] = d_up
            low = dot(d_gate, w_gate[:HALF], 1, 1) + dot(d_up, w_up[:HALF], 1, 1)
            high = dot(d_gate, w_gate[HALF:], 1, 1) + dot(d_up, w_up[HALF:], 1, 1)
            ret_send[m, blocks] = (
                jnp.where(first_rows(low.shape), low, high)
                .astype(BF16)
                .reshape(PART, BLOCK, HALF)
            )
            send_blocks(
                ret_send,
                ret_recv,
                m,
                section,
                ret_send_sem.at[m],
                ret_recv_sem.at[m],
                part * PART,
                PART + part * (PART - 1),
                back=True,
            )
        keep_own(ret_send, ret_recv, m, ret_recv_sem.at[m])

        in_rows = in_recv[m].reshape(SLOTS, HALF)
        cot_rows = cot_recv[m].reshape(SLOTS, HALF)
        left = (lax.broadcasted_iota(jnp.int32, (HIDDEN, SLOTS), 1) % BLOCK) < CAP
        for rows_ref, total, others in (
            (d_gate_rows[...], acc_gate, in_rows),
            (d_up_rows[...], acc_up, in_rows),
            (act[m], acc_down, cot_rows),
        ):
            turned = rows_ref.astype(F32).T
            total[0] += dot(jnp.where(left, turned, 0.0).astype(BF16), others)
            total[1] += dot(jnp.where(left, 0.0, turned).astype(BF16), others)

        if m == MICRO - 1:
            for half in range(2):
                span = pl.ds(half * HALF, HALF)
                grad_gate_ref[span, :] = acc_gate[half].T.astype(BF16)
                grad_up_ref[span, :] = acc_up[half].T.astype(BF16)
                grad_down_ref[:, span] = acc_down[half].astype(BF16)

        @pl.when(jnp.logical_not(is_top))
        def _():
            pltpu.make_async_copy(cot.at[m], cot.at[m], res_recv_sem.at[m]).wait()

        wait_blocks(ret_recv, m, ret_recv_sem.at[m], 0, EXPERTS)
        d_normed = dot(own_from[m], ret_recv[m].reshape(SLOTS, HALF))
        units = unit[m]
        gained = d_normed * units
        gain_part[...] += jnp.concatenate(
            [
                jnp.sum(gained[:ROWS], axis=0, keepdims=True),
                jnp.sum(gained[ROWS:], axis=0, keepdims=True),
            ],
            axis=0,
        )
        gain = jnp.concatenate(
            [
                jnp.broadcast_to(gain_ref[:, :HALF], (ROWS, HALF)),
                jnp.broadcast_to(gain_ref[:, HALF:], (ROWS, HALF)),
            ],
            axis=0,
        )
        scaled = d_normed * gain
        sums = jnp.sum(scaled * units, axis=-1, keepdims=True)
        mean = (sums[:ROWS] + sums[ROWS:]) * (1.0 / WIDTH)
        means = jnp.concatenate([mean, mean], axis=0)
        scales = scale[m][:, :1]
        scales = jnp.concatenate([scales, scales], axis=0)
        grad = (cot[m].astype(F32) + scales * (scaled - units * means)).astype(BF16)
        out_ref[0, m, :, :HALF] = grad[:ROWS]
        out_ref[0, m, :, HALF:] = grad[ROWS:]

        @pl.when(jnp.logical_not(is_last))
        def _():
            for part in range(2):
                span = pl.ds(part * PART * BLOCK, PART * BLOCK)
                cot_send[m, pl.ds(part * PART, PART)] = spread_scaled(
                    next_to[m, span], grad, next_weight[m, span]
                )
                send_blocks(
                    cot_send,
                    cot_recv,
                    m,
                    section - 1,
                    cot_send_sem.at[m],
                    cot_recv_sem.at[m, part],
                    part * PART,
                    PART + part * PART,
                )
            cot_out[m] = grad
            send_one(cot_out.at[m], cot.at[m], section - 1, res_send_sem.at[m], res_recv_sem.at[m])

        if m < MICRO - 1:
            before(m + 1)

        return carry

    for m in range(MICRO):
        one_micro(m, 0)

    gain_all[index] = gain_part[...]

    def send_gain(number, carry):
        pltpu.make_async_remote_copy(
            gain_part,
            gain_all.at[index],
            gain_send_sem,
            gain_recv_sem,
            device_id=(section, peer(number, index)),
            device_id_type=MESH,
        ).start()
        return carry

    lax.fori_loop(0, EXPERTS - 1, send_gain, 0)

    def drain(m, carry):
        wait_blocks(ret_send, m, ret_send_sem.at[m], 0, EXPERTS - 1)

        @pl.when((section < SECTIONS - 2) | (is_top & (m == 0)))
        def _():
            wait_blocks(in_send, m, in_send_sem.at[m], 0, EXPERTS - 1)

        @pl.when(is_top & (m == 0))
        def _():
            wait_blocks(top_send, m, top_send_sem.at[m], 0, EXPERTS - 1)

        @pl.when(is_helper & ((m > 0) | helps_second))
        def _():
            wait_blocks(top_send, m, top_send_sem.at[m], 0, EXPERTS)

        @pl.when(is_second | (is_top & (m > 0)))
        def _():
            pltpu.make_async_copy(normed.at[m], normed.at[m], rows_send_sem.at[m]).wait()

        @pl.when(jnp.logical_not(is_last))
        def _():
            wait_blocks(cot_send, m, cot_send_sem.at[m], 0, EXPERTS)
            pltpu.make_async_copy(cot_out.at[m], cot_out.at[m], res_send_sem.at[m]).wait()

        return carry

    lax.fori_loop(0, MICRO, drain, 0)

    def meta_sent(sem):
        pltpu.make_async_copy(meta_own, meta_own, sem).wait()

    pl.when(jnp.logical_not(is_top))(lambda: meta_sent(meta_send_sem))
    pl.when(is_top | is_second)(lambda: meta_sent(meta_help_send_sem.at[0]))
    pl.when(is_top)(lambda: meta_sent(meta_help_send_sem.at[1]))

    others = gain_all.at[pl.ds(0, EXPERTS - 1)]
    pltpu.make_async_copy(others, others, gain_recv_sem).wait()
    pltpu.make_async_copy(others, others, gain_send_sem).wait()
    total = jnp.sum(gain_all[...], axis=0)
    gain_out_ref[:, :HALF] = total[:1]
    gain_out_ref[:, HALF:] = total[1:]


def local(layer_inputs, expert_ids, gate_weights, norm_gain, w_gate, w_up, w_down, top_cotangent):
    blocks = pltpu.VMEM((MICRO, EXPERTS, BLOCK, HALF), BF16)
    vmem = pl.BlockSpec(memory_space=pltpu.VMEM)
    hbm = pl.BlockSpec(memory_space=pl.ANY)
    dma = pltpu.SemaphoreType.DMA
    outs = pl.pallas_call(
        kernel,
        out_shape=(
            jax.ShapeDtypeStruct((1, MICRO, ROWS, WIDTH), BF16),
            jax.ShapeDtypeStruct((WIDTH, HIDDEN), BF16),
            jax.ShapeDtypeStruct((WIDTH, HIDDEN), BF16),
            jax.ShapeDtypeStruct((HIDDEN, WIDTH), BF16),
            jax.ShapeDtypeStruct((1, WIDTH), F32),
        ),
        in_specs=[vmem] * 5 + [hbm] * 3,
        out_specs=(vmem,) * 5,
        scratch_shapes=[
            pltpu.VMEM((WIDTH, HIDDEN), BF16),
            pltpu.VMEM((WIDTH, HIDDEN), BF16),
            pltpu.VMEM((HIDDEN, WIDTH), BF16),
            pltpu.VMEM((MICRO, 8, 128), F32),
            pltpu.VMEM((MICRO, 8, 128), F32),
            pltpu.VMEM((MICRO, 8, 128), F32),
            pltpu.VMEM((MICRO, SLOTS, 2 * ROWS), BF16),
            pltpu.VMEM((MICRO, 2 * ROWS, SLOTS), BF16),
            pltpu.VMEM((MICRO, SLOTS, 128), F32),
            pltpu.VMEM((MICRO, SLOTS, 2 * ROWS), BF16),
            pltpu.VMEM((MICRO, SLOTS, 128), F32),
            pltpu.VMEM((MICRO, 2 * ROWS, HALF), F32),
            pltpu.VMEM((MICRO, ROWS, 128), F32),
            pltpu.VMEM((MICRO, 2 * ROWS, HALF), BF16),
            pltpu.VMEM((MICRO, 2 * ROWS, HALF), BF16),
            pltpu.VMEM((MICRO, 2 * ROWS, HALF), BF16),
            pltpu.VMEM((MICRO, 2 * ROWS, HALF), BF16),
            blocks,
            blocks,
            blocks,
            blocks,
            blocks,
            blocks,
            blocks,
            pltpu.VMEM((MICRO, SLOTS, HIDDEN), F32),
            pltpu.VMEM((MICRO, SLOTS, HIDDEN), F32),
            pltpu.VMEM((MICRO, SLOTS, HIDDEN), BF16),
            pltpu.VMEM((SLOTS, HIDDEN), BF16),
            pltpu.VMEM((SLOTS, HIDDEN), BF16),
            pltpu.VMEM((2, HIDDEN, HALF), F32),
            pltpu.VMEM((2, HIDDEN, HALF), F32),
            pltpu.VMEM((2, HIDDEN, HALF), F32),
            pltpu.VMEM((2, HALF), F32),
            pltpu.VMEM((EXPERTS, 2, HALF), F32),
            dma((3,)),
            dma,
            dma,
            dma((2,)),
            dma,
            dma((MICRO,)),
            dma((MICRO,)),
            dma((MICRO,)),
            dma((MICRO,)),
            dma((MICRO,)),
            dma((MICRO,)),
            dma((MICRO, 2)),
            dma((MICRO,)),
            dma((MICRO,)),
            dma((MICRO,)),
            dma((MICRO,)),
            dma,
            dma,
        ],
        compiler_params=pltpu.CompilerParams(
            collective_id=0, has_side_effects=True, vmem_limit_bytes=56 * 1024 * 1024
        ),
    )(
        layer_inputs,
        jnp.transpose(expert_ids, (0, 3, 1, 2)),
        jnp.transpose(gate_weights, (0, 3, 1, 2)),
        norm_gain,
        top_cotangent,
        w_gate[0, 0],
        w_up[0, 0],
        w_down[0, 0],
    )
    return (outs[0], outs[1][None, None], outs[2][None, None], outs[3][None, None], outs[4])


def solution(mesh):
    in_specs = (
        P("section", None, "expert", None),
        P("section", None, "expert", None),
        P("section", None, "expert", None),
        P("section", None),
        P("section", "expert", None, None),
        P("section", "expert", None, None),
        P("section", "expert", None, None),
        P(None, "expert", None),
    )
    out_specs = (
        P("section", None, "expert", None),
        P("section", "expert", None, None),
        P("section", "expert", None, None),
        P("section", "expert", None, None),
        P("section", None),
    )
    return jax.shard_map(local, mesh=mesh, in_specs=in_specs, out_specs=out_specs, check_vma=False)
```
